32 devices in a mesh: dp: 4 (over y, core), expert: 8 (over z, x).
Axes of the slice: x: 2, y: 2, z: 4, core: 2. Of those that a mesh axis runs over, the one named last changes fastest.
Arguments:
- tokens: bfloat16 [1024, 2560], P('expert'), may hold values from -6 to 6
- routes: int32 [1024, 6], P('expert'), may hold values from 0 to 7, as said below
- gate_probs: float32 [1024, 6], P('expert'), may hold values from 0.1 to 1
- shadow: int32 [1], replicated, may hold values from 0 to 7, as said below
- w_gate: bfloat16 [8, 1536, 2560], P('expert', 'dp'), may hold values from -0.125 to 0.125
- w_up: bfloat16 [8, 1536, 2560], P('expert', 'dp'), may hold values from -0.125 to 0.125
- w_down: bfloat16 [8, 1536, 2560], P('expert', 'dp'), may hold values from -0.15625 to 0.15625
- cotangent: bfloat16 [1024, 2560], P('expert'), may hold values from -6 to 6
Outputs:
- layer_out: bfloat16 [1024, 2560], P('expert', 'dp')
- grad_tokens: bfloat16 [1024, 2560], P('expert', 'dp')
- grad_gate: bfloat16 [8, 1536, 2560], P('expert', 'dp')
- grad_up: bfloat16 [8, 1536, 2560], P('expert', 'dp')
- grad_down: bfloat16 [8, 1536, 2560], P('expert', 'dp')
The draws below stay inside these ranges and needn't reach their ends.
Inputs may be any that keep to these rules, and one draw needn't show every extreme that they name: `routes`: each row names 6 different experts. `shadow`: an expert id.
All inputs are finite; a program needn't handle non-finite values.
Results may differ from the reference program's by a relative error of at most 0.012.
Values may be sent and summed in bfloat16 or wider, within the bound.
A program may use at most 192 MiB of HBM per device.

```python
import jax
import jax.numpy as jnp
from jax import lax

D = 2560
FF = 1536
TOP = 6
TOK_DEV = 128
EXPERTS = 8
CAP = 96
TOKENS = 1024
N_DP = 4
N_EXPERT = 8


def route_plan(key):
    expert_order = jax.random.permutation(jax.random.fold_in(key, 11), EXPERTS).astype(jnp.int32)
    rank_of = jnp.zeros((EXPERTS,), jnp.int32).at[expert_order].set(jnp.arange(EXPERTS, dtype=jnp.int32))
    scores = jax.random.randint(jax.random.fold_in(key, 12), (TOKENS, EXPERTS), 0, 1000, dtype=jnp.int32)
    position = jnp.arange(TOKENS, dtype=jnp.int32) % TOK_DEV
    early_token = (position <= CAP)[:, None]
    crowded = jnp.logical_and(rank_of >= 1, rank_of <= 2)[None, :]
    score_bias = jnp.where(rank_of == 0, 800, 0)[None, :] + jnp.where(crowded, jnp.where(early_token, 3000, 500), 0)
    ranked_score = (scores + score_bias) * EXPERTS + jnp.arange(EXPERTS, dtype=jnp.int32)[None, :]
    chosen = lax.top_k(ranked_score, TOP)[1].astype(jnp.int32)
    return (chosen, expert_order[:1])


def draw_routes(key, part):
    chosen, picked = route_plan(key)
    return chosen


def draw_shadow(key, part):
    chosen, picked = route_plan(key)
    return picked


def steps_of(own_key, dims, cuts, low, high):
    level = 1.0
    for dim, blocks in cuts:
        steps = jax.random.uniform(jax.random.fold_in(jax.random.fold_in(own_key, 6), dim), (blocks,), jnp.float32, low / len(cuts), high / len(cuts))
        level = level * jnp.repeat(jnp.exp(steps), dims[dim] // blocks).reshape((-1,) + (1,) * (len(dims) - 1 - dim))
    return level


def normal_values(rng, shape, deviation, reach, pieces=(), kind=jnp.bfloat16):
    level = steps_of(rng, shape, pieces, -0.22, 0.18) if pieces else 1.0
    entries = jax.random.normal(rng, shape, jnp.float32) * deviation * level
    return jnp.minimum(jnp.maximum(entries, -reach), reach).astype(kind)


def setup_inputs(seed: int = 0) -> dict:
    key_of = jax.random.split(jax.random.key(seed), 9)
    return {
        "tokens": normal_values(key_of[0], (TOKENS, D), 1.0, 6.0, ((0, 8),)),
        "routes": draw_routes(jax.random.fold_in(key_of[8], 71), 0),
        "gate_probs": jnp.clip(0.1 + 0.9 * jax.random.uniform(key_of[2], (TOKENS, TOP), jnp.float32) ** steps_of(key_of[2], (TOKENS, TOP), ((0, 8),), -0.2, 0.2), 0.1, 1.0),
        "shadow": draw_shadow(jax.random.fold_in(key_of[8], 71), 0),
        "w_gate": normal_values(key_of[4], (EXPERTS, FF, D), D ** -0.5, 0.125, ((0, 8), (1, 4))),
        "w_up": normal_values(key_of[5], (EXPERTS, FF, D), D ** -0.5, 0.125, ((0, 8), (1, 4))),
        "w_down": normal_values(key_of[6], (EXPERTS, FF, D), FF ** -0.5, 0.15625, ((0, 8), (1, 4))),
        "cotangent": normal_values(key_of[7], (TOKENS, D), 1.0, 6.0, ((0, 8),)),
    }


def rounded(numbers):
    return lax.optimization_barrier(numbers.astype(jnp.bfloat16))


def expert_rows(rows_x, rows_c, gate_w, up_w, down_w):
    contract = (((1,), (1,)), ((), ()))
    hidden = lax.dot_general(rows_x, gate_w, contract, preferred_element_type=jnp.float32)
    up_value = lax.dot_general(rows_x, up_w, contract, preferred_element_type=jnp.float32)
    gate_sigmoid = jax.nn.sigmoid(hidden)
    gated_hidden = hidden * gate_sigmoid
    active = rounded(gated_hidden * up_value)
    back_hidden = lax.dot_general(rows_c, down_w, contract, preferred_element_type=jnp.float32)
    d_hidden = rounded(back_hidden * up_value * gate_sigmoid * (1.0 + hidden * (1.0 - gate_sigmoid)))
    d_up = rounded(back_hidden * gated_hidden)
    return active, d_hidden, d_up


def outer_sums(active, d_hidden, d_up, rows_x, rows_c):
    over_rows = (((0,), (0,)), ((), ()))
    return (lax.dot_general(d_hidden, rows_x, over_rows, preferred_element_type=jnp.float32),
            lax.dot_general(d_up, rows_x, over_rows, preferred_element_type=jnp.float32),
            lax.dot_general(active, rows_c, over_rows, preferred_element_type=jnp.float32))


def grouped_terms(active, d_hidden, d_up, gate_w, up_w, down_w):
    group_width = FF // N_DP
    row_total = active.shape[0]
    out_total = jnp.zeros((row_total, D), jnp.float32)
    back_total = jnp.zeros((row_total, D), jnp.float32)
    for group_index in range(N_DP):
        lower_edge = group_index * group_width
        upper_edge = lower_edge + group_width
        partial_value = jnp.dot(active[:, lower_edge:upper_edge], down_w[lower_edge:upper_edge], preferred_element_type=jnp.float32)
        out_total = out_total + rounded(partial_value).astype(jnp.float32)
        partial_value = jnp.dot(d_hidden[:, lower_edge:upper_edge], gate_w[lower_edge:upper_edge], preferred_element_type=jnp.float32)
        partial_value = partial_value + jnp.dot(d_up[:, lower_edge:upper_edge], up_w[lower_edge:upper_edge], preferred_element_type=jnp.float32)
        back_total = back_total + rounded(partial_value).astype(jnp.float32)
    return rounded(out_total), rounded(back_total)


def reference(tokens, routes, gate_probs, shadow, w_gate, w_up, w_down, cotangent):
    blocks = N_EXPERT
    pair_count = TOK_DEV * TOP
    slot_count = blocks * CAP
    flattened = routes.reshape(blocks, pair_count)
    onehot = (flattened[:, :, None] == jnp.arange(EXPERTS, dtype=jnp.int32)[None, None, :]).astype(jnp.int32)
    earlier = jnp.sum((jnp.cumsum(onehot, axis=1) - onehot) * onehot, axis=2)
    target = shadow[0]
    kept_pair = jnp.logical_and(flattened != target, earlier < CAP)
    block_ids = jnp.arange(blocks, dtype=jnp.int32)[:, None]
    pair_ids = block_ids * pair_count + jnp.arange(pair_count, dtype=jnp.int32)[None, :]
    column = block_ids * CAP + earlier
    row_target = jnp.where(kept_pair, flattened, EXPERTS)
    slot_table = jnp.full((EXPERTS, slot_count), -1, jnp.int32)
    slot_table = slot_table.at[row_target.reshape(-1), column.reshape(-1)].set(pair_ids.reshape(-1), mode="drop")
    prob_flat = gate_probs.reshape(-1)

    def one_expert(inputs):
        expert_index, gate_w, up_w, down_w = inputs
        pair_index = slot_table[expert_index]
        usable = pair_index >= 0
        clamped = jnp.maximum(pair_index, 0)
        token_index = clamped // TOP
        rows_x = jnp.where(usable[:, None], tokens[token_index], jnp.zeros((), jnp.bfloat16))
        weight = jnp.where(usable, prob_flat[clamped], jnp.zeros((), jnp.float32))
        rows_c = (weight[:, None] * cotangent[token_index].astype(jnp.float32)).astype(jnp.bfloat16)
        active, d_hidden, d_up = expert_rows(rows_x, rows_c, gate_w, up_w, down_w)
        out_rows, back_rows = grouped_terms(active, d_hidden, d_up, gate_w, up_w, down_w)
        gradients = outer_sums(active, d_hidden, d_up, rows_x, rows_c)
        return (out_rows, back_rows, gradients[0].astype(jnp.bfloat16),
                gradients[1].astype(jnp.bfloat16), gradients[2].astype(jnp.bfloat16))

    out_rows, back_rows, grad_gate, grad_up, grad_down = lax.map(
        one_expert, (jnp.arange(EXPERTS, dtype=jnp.int32), w_gate, w_up, w_down))

    position = jnp.where(kept_pair, flattened * slot_count + column, 0).reshape(TOKENS, TOP)
    kept_tokens = kept_pair.reshape(TOKENS, TOP)
    picked_out = out_rows.reshape(EXPERTS * slot_count, D)[position]
    picked_back = back_rows.reshape(EXPERTS * slot_count, D)[position]
    weight = jnp.where(kept_tokens, gate_probs, jnp.zeros((), jnp.float32))
    mixed_sum = jnp.sum(weight[:, :, None] * picked_out.astype(jnp.float32), axis=1)
    back_sum = jnp.sum(jnp.where(kept_tokens[:, :, None], picked_back.astype(jnp.float32), jnp.zeros((), jnp.float32)), axis=1)

    shadow_share = jnp.sum(jnp.where(routes == target, gate_probs, jnp.zeros((), jnp.float32)), axis=1)
    shadow_c = (shadow_share[:, None] * cotangent.astype(jnp.float32)).astype(jnp.bfloat16)
    gate_s = w_gate[target]
    up_s = w_up[target]
    down_s = w_down[target]
    active_s, d_hidden_s, d_up_s = expert_rows(tokens, shadow_c, gate_s, up_s, down_s)
    out_s, back_s = grouped_terms(active_s, d_hidden_s, d_up_s, gate_s, up_s, down_s)
    layer_out = (mixed_sum + shadow_share[:, None] * out_s.astype(jnp.float32)).astype(jnp.bfloat16)
    grad_tokens = (back_sum + back_s.astype(jnp.float32)).astype(jnp.bfloat16)

    def block_rows(matrix, block_index):
        grid = matrix.reshape(N_EXPERT, TOK_DEV, matrix.shape[1])
        return lax.dynamic_index_in_dim(grid, block_index, axis=0, keepdims=False)

    def add_block(running, block_index):
        gradients = outer_sums(block_rows(active_s, block_index), block_rows(d_hidden_s, block_index),
                               block_rows(d_up_s, block_index), block_rows(tokens, block_index),
                               block_rows(shadow_c, block_index))
        updated = (running[0] + rounded(gradients[0]).astype(jnp.float32),
                   running[1] + rounded(gradients[1]).astype(jnp.float32),
                   running[2] + rounded(gradients[2]).astype(jnp.float32))
        return updated, None

    zero_grad = jnp.zeros((FF, D), jnp.float32)
    shadow_grads, unused = lax.scan(add_block, (zero_grad, zero_grad, zero_grad), jnp.arange(N_EXPERT, dtype=jnp.int32))
    grad_gate = grad_gate.at[target].set(shadow_grads[0].astype(jnp.bfloat16))
    grad_up = grad_up.at[target].set(shadow_grads[1].astype(jnp.bfloat16))
    grad_down = grad_down.at[target].set(shadow_grads[2].astype(jnp.bfloat16))
    return layer_out, grad_tokens, grad_gate, grad_up, grad_down
```

```python
import jax
import jax.numpy as jnp
from jax import lax
from jax.sharding import PartitionSpec as P

F32 = jnp.float32
BF16 = jnp.bfloat16
BOTH = ("expert", "dp")


def route_weights(routes, gate_probs, target, n_exp):
    token_count, top = routes.shape
    capacity = max(2, token_count * top // n_exp)
    experts = lax.broadcasted_iota(jnp.int32, (1, 1, n_exp), 2)
    match = routes[:, :, None] == experts
    prob = jnp.sum(jnp.where(match, gate_probs[:, :, None], 0.0), axis=1)
    hit = jnp.any(match, axis=1)
    row = lax.broadcasted_iota(jnp.int32, (token_count, token_count), 0)
    col = lax.broadcasted_iota(jnp.int32, (token_count, token_count), 1)
    earlier = jnp.dot((col < row).astype(BF16), hit.astype(BF16), preferred_element_type=F32)
    open_slot = jnp.logical_or(experts[0] == target, earlier < capacity)
    return jnp.where(jnp.logical_and(hit, open_slot), prob, 0.0)


def body(tokens, routes, gate_probs, shadow, w_gate, w_up, w_down, cotangent):
    n_exp = lax.axis_size("expert")
    n_dp = lax.axis_size("dp")
    token_count, width = tokens.shape
    part = token_count // n_dp
    dp = lax.axis_index("dp")
    expert = lax.axis_index("expert")
    weights = route_weights(routes, gate_probs, shadow[0], n_exp)
    mine = jnp.stack(
        [
            lax.dynamic_slice_in_dim(tokens, dp * part, part, 0),
            lax.dynamic_slice_in_dim(cotangent, dp * part, part, 0),
        ]
    )
    all_w = lax.all_gather(weights, "expert", axis=0, tiled=True)
    w = lax.dynamic_slice_in_dim(all_w, expert, 1, 1)
    both = lax.all_gather(mine, BOTH, axis=1, tiled=True)
    x = both[0]
    c = (w * both[1].astype(F32)).astype(BF16)
    gate_w, up_w, down_w = w_gate[0], w_up[0], w_down[0]
    contract = (((1,), (1,)), ((), ()))
    hidden = lax.dot_general(x, gate_w, contract, preferred_element_type=F32)
    up = lax.dot_general(x, up_w, contract, preferred_element_type=F32)
    back = lax.dot_general(c, down_w, contract, preferred_element_type=F32)
    sig = jax.nn.sigmoid(hidden)
    gated = hidden * sig
    active = (gated * up).astype(BF16)
    d_hidden = (back * up * sig * (1.0 + hidden * (1.0 - sig))).astype(BF16)
    d_up = (back * gated).astype(BF16)
    out = (w * jnp.dot(active, down_w, preferred_element_type=F32)).astype(BF16)
    back_rows = (
        jnp.dot(d_hidden, gate_w, preferred_element_type=F32)
        + jnp.dot(d_up, up_w, preferred_element_type=F32)
    ).astype(BF16)

    def chunks(value):
        value = value.reshape(n_exp, token_count, n_dp, width // n_dp)
        return value.transpose(0, 2, 1, 3)

    partial = jnp.stack([chunks(out), chunks(back_rows)], axis=2)
    partial = partial.reshape(n_exp * n_dp * 2 * token_count, width // n_dp)
    summed = lax.psum_scatter(partial, BOTH, scatter_dimension=0, tiled=True)
    over_rows = (((0,), (0,)), ((), ()))
    grads = [
        lax.dot_general(left, right, over_rows, preferred_element_type=F32).astype(BF16)[None]
        for left, right in ((d_hidden, x), (d_up, x), (active, c))
    ]
    summed = summed.reshape(2, token_count, width // n_dp)
    return (summed[0], summed[1], *grads)


def solution(mesh):
    rows = P("expert", None)
    split = P("expert", "dp", None)
    return jax.shard_map(
        body,
        mesh=mesh,
        in_specs=(rows, rows, rows, P(), split, split, split, rows),
        out_specs=(P("expert", "dp"), P("expert", "dp"), split, split, split),
        check_vma=False,
    )
```

```python
import jax
import jax.numpy as jnp
from jax import lax
from jax.sharding import PartitionSpec as P

F32 = jnp.float32
BF16 = jnp.bfloat16
BOTH = ("expert", "dp")


def route_weights(routes, gate_probs, target, n_exp):
    token_count, top = routes.shape
    capacity = max(2, token_count * top // n_exp)
    experts = lax.broadcasted_iota(jnp.int32, (1, 1, n_exp), 2)
    match = routes[:, :, None] == experts
    prob = jnp.sum(jnp.where(match, gate_probs[:, :, None], 0.0), axis=1)
    hit = jnp.any(match, axis=1)
    row = lax.broadcasted_iota(jnp.int32, (token_count, token_count), 0)
    col = lax.broadcasted_iota(jnp.int32, (token_count, token_count), 1)
    earlier = jnp.dot((col < row).astype(BF16), hit.astype(BF16), preferred_element_type=F32)
    open_slot = jnp.logical_or(experts[0] == target, earlier < capacity)
    return jnp.where(jnp.logical_and(hit, open_slot), prob, 0.0)


def swap(value, axis, bit):
    size = lax.axis_size(axis)
    return lax.ppermute(value, axis, [(i, i ^ (1 << bit)) for i in range(size)])


def add(left, right):
    return (left.astype(F32) + right.astype(F32)).astype(BF16)


def halve(parts, stages, ex_bits):
    left = list(range(ex_bits - 1, -1, -1))
    for axis, bit in stages:
        if axis == "dp":
            mask = 1 << bit
            parts = {
                j: add(value, swap(parts[j ^ mask], axis, bit))
                for j, value in parts.items()
                if not j & mask
            }
        else:
            place = left.index(bit)
            left.remove(bit)
            mine = (lax.axis_index(axis) >> bit) % 2
            parts = {
                j: add(
                    lax.dynamic_index_in_dim(value, mine, place, keepdims=False),
                    swap(
                        lax.dynamic_index_in_dim(value, 1 - mine, place, keepdims=False),
                        axis,
                        bit,
                    ),
                )
                for j, value in parts.items()
            }
    return parts[0]


def body(tokens, routes, gate_probs, shadow, w_gate, w_up, w_down, cotangent):
    n_exp = lax.axis_size("expert")
    n_dp = lax.axis_size("dp")
    token_count, width = tokens.shape
    part = token_count // n_dp
    dp = lax.axis_index("dp")
    expert = lax.axis_index("expert")
    weights = route_weights(routes, gate_probs, shadow[0], n_exp)
    mine = jnp.stack(
        [
            lax.dynamic_slice_in_dim(tokens, dp * part, part, 0),
            lax.dynamic_slice_in_dim(cotangent, dp * part, part, 0),
        ]
    )
    all_w = lax.all_gather(weights, "expert", axis=0, tiled=True)
    w = lax.dynamic_slice_in_dim(all_w, expert, 1, 1)
    both = lax.all_gather(mine, BOTH, axis=1, tiled=True)
    x = both[0]
    c = (w * both[1].astype(F32)).astype(BF16)
    gate_w, up_w, down_w = w_gate[0], w_up[0], w_down[0]
    contract = (((1,), (1,)), ((), ()))
    hidden = lax.dot_general(x, gate_w, contract, preferred_element_type=F32)
    up = lax.dot_general(x, up_w, contract, preferred_element_type=F32)
    back = lax.dot_general(c, down_w, contract, preferred_element_type=F32)
    sig = jax.nn.sigmoid(hidden)
    gated = hidden * sig
    active = (gated * up).astype(BF16)
    d_hidden = (back * up * sig * (1.0 + hidden * (1.0 - sig))).astype(BF16)
    d_up = (back * gated).astype(BF16)
    cols = width // n_dp
    dp_bits, ex_bits = n_dp.bit_length() - 1, n_exp.bit_length() - 1
    blocks = (2,) * ex_bits + (token_count, cols)
    out_parts, back_parts = {}, {}
    order = sorted(range(n_dp), key=lambda j: (1 - j % 2, j))
    for j in order:
        start = jnp.bitwise_xor(dp, j) * cols
        cut = [lax.dynamic_slice_in_dim(m, start, cols, 1) for m in (gate_w, up_w, down_w)]
        value = w * jnp.dot(active, cut[2], preferred_element_type=F32)
        out_parts[j] = value.astype(BF16).reshape(blocks)
        value = jnp.dot(d_hidden, cut[0], preferred_element_type=F32)
        value = value + jnp.dot(d_up, cut[1], preferred_element_type=F32)
        back_parts[j] = value.astype(BF16).reshape(blocks)
    rest_dp = [("dp", b) for b in range(1, dp_bits)]
    rest_ex = [("expert", b) for b in range(1, ex_bits)]
    layer_out = halve(out_parts, [("dp", 0), *rest_dp, ("expert", 0), *rest_ex], ex_bits)
    grad_tokens = halve(back_parts, [("dp", 0), ("expert", 0), *rest_dp, *rest_ex], ex_bits)
    over_rows = (((0,), (0,)), ((), ()))
    grads = [
        lax.dot_general(left, right, over_rows, preferred_element_type=F32).astype(BF16)[None]
        for left, right in ((d_hidden, x), (d_up, x), (active, c))
    ]
    return (layer_out, grad_tokens, *grads)


def solution(mesh):
    rows = P("expert", None)
    split = P("expert", "dp", None)
    return jax.shard_map(
        body,
        mesh=mesh,
        in_specs=(rows, rows, rows, P(), split, split, split, rows),
        out_specs=(P("expert", "dp"), P("expert", "dp"), split, split, split),
        check_vma=False,
    )
```

```python
import jax
import jax.numpy as jnp
from jax import lax
from jax.sharding import PartitionSpec as P

F32 = jnp.float32
BF16 = jnp.bfloat16
BOTH = ("expert", "dp")


def route_weights(routes, gate_probs, target, n_exp):
    token_count, top = routes.shape
    capacity = max(2, token_count * top // n_exp)
    experts = lax.broadcasted_iota(jnp.int32, (1, 1, n_exp), 2)
    match = routes[:, :, None] == experts
    prob = jnp.sum(jnp.where(match, gate_probs[:, :, None], 0.0), axis=1)
    hit = jnp.any(match, axis=1)
    row = lax.broadcasted_iota(jnp.int32, (token_count, token_count), 0)
    col = lax.broadcasted_iota(jnp.int32, (token_count, token_count), 1)
    earlier = jnp.dot((col < row).astype(BF16), hit.astype(BF16), preferred_element_type=F32)
    open_slot = jnp.logical_or(experts[0] == target, earlier < capacity)
    return jnp.where(jnp.logical_and(hit, open_slot), prob, 0.0)


def swap(value, axis, bit):
    size = lax.axis_size(axis)
    return lax.ppermute(value, axis, [(i, i ^ (1 << bit)) for i in range(size)])


def add(left, right):
    return (left.astype(F32) + right.astype(F32)).astype(BF16)


def halve(parts, stages, ex_bits):
    left = list(range(ex_bits - 1, -1, -1))
    for axis, bit in stages:
        if axis == "dp":
            mask = 1 << bit
            parts = {
                j: add(value, swap(parts[j ^ mask], axis, bit))
                for j, value in parts.items()
                if not j & mask
            }
        else:
            place = left.index(bit)
            left.remove(bit)
            mine = (lax.axis_index(axis) >> bit) % 2
            parts = {
                j: add(
                    lax.dynamic_index_in_dim(value, mine, place, keepdims=False),
                    swap(
                        lax.dynamic_index_in_dim(value, 1 - mine, place, keepdims=False),
                        axis,
                        bit,
                    ),
                )
                for j, value in parts.items()
            }
    return parts[0]


def body(tokens, routes, gate_probs, shadow, w_gate, w_up, w_down, cotangent):
    n_exp = lax.axis_size("expert")
    n_dp = lax.axis_size("dp")
    token_count, width = tokens.shape
    part = token_count // n_dp
    dp = lax.axis_index("dp")
    expert = lax.axis_index("expert")
    weights = route_weights(routes, gate_probs, shadow[0], n_exp)
    mine = jnp.stack(
        [
            lax.dynamic_slice_in_dim(tokens, dp * part, part, 0),
            lax.dynamic_slice_in_dim(cotangent, dp * part, part, 0),
        ]
    )
    all_w = lax.all_gather(weights, "expert", axis=0, tiled=True)
    w = lax.dynamic_slice_in_dim(all_w, expert, 1, 1)
    both = lax.all_gather(mine, BOTH, axis=1, tiled=True)
    x = both[0]
    c = (w * both[1].astype(F32)).astype(BF16)
    gate_w, up_w, down_w = w_gate[0], w_up[0], w_down[0]
    contract = (((1,), (1,)), ((), ()))
    hidden = lax.dot_general(x, gate_w, contract, preferred_element_type=F32)
    up = lax.dot_general(x, up_w, contract, preferred_element_type=F32)
    back = lax.dot_general(c, down_w, contract, preferred_element_type=F32)
    sig = jax.nn.sigmoid(hidden)
    gated = hidden * sig
    active = (gated * up).astype(BF16)
    d_hidden = (back * up * sig * (1.0 + hidden * (1.0 - sig))).astype(BF16)
    d_up = (back * gated).astype(BF16)
    cols = width // n_dp
    dp_bits, ex_bits = n_dp.bit_length() - 1, n_exp.bit_length() - 1
    blocks = (2,) * ex_bits + (token_count, cols)
    out_parts, back_parts = {}, {}
    order = sorted(range(n_dp), key=lambda j: (1 - j % 2, j))
    for j in order:
        start = jnp.bitwise_xor(dp, j) * cols
        cut = [lax.dynamic_slice_in_dim(m, start, cols, 1) for m in (gate_w, up_w, down_w)]
        value = w * jnp.dot(active, cut[2], preferred_element_type=F32)
        out_parts[j] = value.astype(BF16).reshape(blocks)
        value = jnp.dot(d_hidden, cut[0], preferred_element_type=F32)
        value = value + jnp.dot(d_up, cut[1], preferred_element_type=F32)
        back_parts[j] = value.astype(BF16).reshape(blocks)
    rest_dp = [("dp", b) for b in range(1, dp_bits)]
    rest_ex = [("expert", b) for b in range(1, ex_bits)]
    d_hidden, d_up, active, out_parts[0], back_parts[0] = lax.optimization_barrier(
        (d_hidden, d_up, active, out_parts[0], back_parts[0])
    )
    layer_out = halve(out_parts, [("dp", 0), *rest_dp, ("expert", 0), *rest_ex], ex_bits)
    grad_tokens = halve(back_parts, [("dp", 0), ("expert", 0), *rest_dp, *rest_ex], ex_bits)
    over_rows = (((0,), (0,)), ((), ()))
    grads = [
        lax.dot_general(left, right, over_rows, preferred_element_type=F32).astype(BF16)[None]
        for left, right in ((d_hidden, x), (d_up, x), (active, c))
    ]
    return (layer_out, grad_tokens, *grads)


def solution(mesh):
    rows = P("expert", None)
    split = P("expert", "dp", None)
    return jax.shard_map(
        body,
        mesh=mesh,
        in_specs=(rows, rows, rows, P(), split, split, split, rows),
        out_specs=(P("expert", "dp"), P("expert", "dp"), split, split, split),
        check_vma=False,
    )
```
